32 devices in a mesh: dp: 8 (over z, y), task: 4 (over x, core).
Axes of the slice: x: 2, y: 2, z: 4, core: 2. Of those that a mesh axis runs over, the one named last changes fastest.
Arguments:
- inputs: bfloat16 [8, 32, 48, 512], P('dp', None, None, 'task'), may hold values from -18 to 18
- extents: int32 [8, 2], P('dp'), may hold values from 1 to 48, as said below
- conflicts: int32 [4, 4], replicated, may hold values 0 or 1
- trunk_weight: float32 [9, 512, 512], P(None, 'dp', 'task'), may hold values from -0.09375 to 0.09375
- attn_first: float32 [4, 512, 512], P('task', 'dp'), may hold values from -0.25 to 0.25
- attn_second: float32 [4, 512, 512], P('task', 'dp'), may hold values from -0.25 to 0.25
- branch_conv: float32 [4, 9, 512, 512], P('task', None, 'dp'), may hold values from -0.09375 to 0.09375
- trunk_momentum: float32 [9, 512, 512], P(None, 'dp', 'task'), may hold values from -64 to 64
- first_momentum: float32 [4, 512, 512], P('task', 'dp'), may hold values from -64 to 64
- second_momentum: float32 [4, 512, 512], P('task', 'dp'), may hold values from -64 to 64
- conv_momentum: float32 [4, 9, 512, 512], P('task', None, 'dp'), may hold values from -64 to 64
- cotangent: bfloat16 [4, 8, 16, 24, 512], P('task', 'dp'), may hold values from -6 to 6
Outputs:
- features: bfloat16 [4, 8, 16, 24, 512], P('task', 'dp')
- input_grad: float32 [8, 32, 48, 512], P('dp', None, None, 'task')
- trunk_weight_new: float32 [9, 512, 512], P(None, 'dp', 'task')
- attn_first_new: float32 [4, 512, 512], P('task', 'dp')
- attn_second_new: float32 [4, 512, 512], P('task', 'dp')
- branch_conv_new: float32 [4, 9, 512, 512], P('task', None, 'dp')
- trunk_momentum_new: float32 [9, 512, 512], P(None, 'dp', 'task')
- first_momentum_new: float32 [4, 512, 512], P('task', 'dp')
- second_momentum_new: float32 [4, 512, 512], P('task', 'dp')
- conv_momentum_new: float32 [4, 9, 512, 512], P('task', None, 'dp')
- task_gram: float32 [4, 4], replicated
The draws below stay inside these ranges and needn't reach their ends.
Inputs may be any that keep to these rules, and one draw needn't show every extreme that they name: Image i's valid pixels are its rows below extents[i, 0] and its columns below extents[i, 1]; extents[i, 0] <= 32 and extents[i, 1] <= 48.
All inputs are finite; a program needn't handle non-finite values.
Results may differ from the reference program's by a relative error of at most 0.0095.
Values may be sent and summed in bfloat16 or wider, within the bound.
No kernel may reach another device: no remote copies, remote signals or barrier semaphores. Data moves between devices by JAX's collectives and lax.ppermute only.
A program may use at most 192 MiB of HBM per device.

```python
import functools
import jax
import jax.numpy as jnp
from jax import lax

C = 512
KK = 9
H = 32
W = 48
NS_STEPS = 3
IMAGES = 8
TASKS = 4


def draw_inputs(key, part):
    key = jax.random.fold_in(key, 5)
    channel_pos = jnp.arange(C, dtype=jnp.float32) / jnp.float32(max(C - 1, 1))
    values = jnp.clip(jax.random.normal(key, (IMAGES, H, W, C), jnp.float32), -6.0, 6.0)
    scales = 1.0 + 2.0 * channel_pos
    return (values * scales).astype(jnp.bfloat16)


def draw_extents(key, part):
    key = jax.random.fold_in(key, 11)
    key_h, key_w = jax.random.split(key)
    ordinal = jnp.arange(IMAGES, dtype=jnp.int32)
    low_h = jnp.maximum(H * (4 * IMAGES + 5 * ordinal) // (10 * IMAGES), 1)
    high_h = jnp.minimum(low_h + H // 10 + 1, H)
    low_w = jnp.maximum(W * (4 * IMAGES + 5 * ordinal) // (10 * IMAGES), 1)
    high_w = jnp.minimum(low_w + W // 10 + 1, W)
    heights = jax.random.randint(key_h, (IMAGES,), low_h, high_h + 1)
    widths = jax.random.randint(key_w, (IMAGES,), low_w, high_w + 1)
    last_one = ordinal == IMAGES - 1
    heights = jnp.where(last_one, H, heights)
    widths = jnp.where(last_one, W, widths)
    return jnp.stack([heights, widths], axis=1).astype(jnp.int32)


def with_ends(values, key, least, top_value):
    extent = values.shape
    place = [jax.random.randint(jax.random.fold_in(key, axis), (), 0, extent[axis]) for axis in range(len(extent))]
    values = values.at[tuple(place)].set(least)
    longest = extent.index(max(extent))
    place[longest] = (place[longest] + 1) % extent[longest]
    return values.at[tuple(place)].set(top_value)


def levels(own_key, dims, cuts, least, high):
    def one(axis_at, blocks):
        steps = jax.random.uniform(jax.random.fold_in(jax.random.fold_in(own_key, 6), axis_at), (blocks,), jnp.float32, least / len(cuts), high / len(cuts))
        return jnp.repeat(jnp.exp(steps), dims[axis_at] // blocks).reshape((-1,) + (1,) * (len(dims) - axis_at - 1))

    level = one(*cuts[0])
    for cut in cuts[1:]:
        level = level * one(*cut)
    return level


def centred(key, dims, deviation, limit, shards=(), held_as=jnp.bfloat16):
    entries = deviation * jax.random.normal(key, dims, jnp.float32)
    if shards:
        entries = entries * levels(key, dims, shards, -0.22, 0.18)
    return jnp.clip(entries, -limit, limit).astype(held_as)


def setup_inputs(seed: int = 0) -> dict:
    keys = jax.random.split(jax.random.key(seed), 13)
    inputs = draw_inputs(jax.random.fold_in(keys[12], 71), 0)
    extents = draw_extents(jax.random.fold_in(keys[12], 71), 0)
    conflicts = with_ends((jax.random.randint(keys[2], (TASKS, TASKS), 0, 2) < 1).astype(jnp.int32), jax.random.fold_in(keys[2], 1), 0, 1)
    trunk_weight = centred(keys[3], (KK, C, C), (KK * C) ** -0.5, 0.09375, ((1, 8), (2, 4)), jnp.float32)
    attn_first = centred(keys[4], (TASKS, C, C), C ** -0.5, 0.25, ((0, 4), (1, 8)), jnp.float32)
    attn_second = centred(keys[5], (TASKS, C, C), C ** -0.5, 0.25, ((0, 4), (1, 8)), jnp.float32)
    branch_conv = centred(keys[6], (TASKS, KK, C, C), (KK * C) ** -0.5, 0.09375, ((0, 4), (2, 8)), jnp.float32)
    trunk_momentum = centred(keys[7], (KK, C, C), (0.1 * (IMAGES * H * W) ** 0.5), 64.0, ((1, 8), (2, 4)), jnp.float32)
    first_momentum = centred(keys[8], (TASKS, C, C), (0.1 * (IMAGES * H * W) ** 0.5), 64.0, ((0, 4), (1, 8)), jnp.float32)
    second_momentum = centred(keys[9], (TASKS, C, C), (0.1 * (IMAGES * H * W) ** 0.5), 64.0, ((0, 4), (1, 8)), jnp.float32)
    conv_momentum = centred(keys[10], (TASKS, KK, C, C), (0.1 * (IMAGES * H * W) ** 0.5), 64.0, ((0, 4), (2, 8)), jnp.float32)
    cotangent = centred(keys[11], (TASKS, IMAGES, H // 2, W // 2, C), 1.0, 6.0, ((0, 4), (1, 8)))
    return {"inputs": inputs, "extents": extents, "conflicts": conflicts, "trunk_weight": trunk_weight, "attn_first": attn_first, "attn_second": attn_second, "branch_conv": branch_conv, "trunk_momentum": trunk_momentum, "first_momentum": first_momentum, "second_momentum": second_momentum, "conv_momentum": conv_momentum, "cotangent": cotangent}


epsilon = 1e-05
moment_decay = 0.95
step_rate = 1.0
weight_decay = 0.01
coeff_a = 3.4445
coeff_b = -4.775
coeff_c = 2.0315
highest = lax.Precision.HIGHEST

@jax.custom_vjp
def low(v):
    return lax.optimization_barrier(v.astype(jnp.bfloat16)).astype(jnp.float32)

@jax.custom_vjp
def low_back(v):
    return v

def low_keep(v):
    return (low(v), None)

def low_pass(kept, grad):
    return (grad,)

def back_keep(v):
    return (v, None)

def back_low(kept, grad):
    return (low(grad),)
low.defvjp(low_keep, low_pass)
low_back.defvjp(back_keep, back_low)

def conv_three(values, kernel):
    height, across = (values.shape[1], values.shape[2])
    padded = jnp.pad(values, ((0, 0), (1, 1), (1, 1), (0, 0)))
    running = jnp.zeros(values.shape[:3] + (kernel.shape[2],), jnp.float32)
    for offset in range(9):
        row_off, col_off = (offset // 3, offset % 3)
        window = padded[:, row_off:row_off + height, col_off:col_off + across]
        running = running + jnp.einsum('ihwc,co->ihwo', window, kernel[offset], precision=highest)
    return running

def batch_norm(values, mask, valid_count):
    average = lax.optimization_barrier(jnp.sum(values * mask, axis=(0, 1, 2))) / valid_count
    second = lax.optimization_barrier(jnp.sum(values * values * mask, axis=(0, 1, 2))) / valid_count
    spread = second - average * average
    return (values - average) * lax.rsqrt(spread + epsilon)

def branch_forward(raw_inputs, trunk_w, first_w, second_w, conv_w, mask, valid_count):
    masked = raw_inputs * mask
    trunk_pre = low_back(conv_three(masked, low(trunk_w)))
    shared = low(low_back(mask * jax.nn.silu(batch_norm(trunk_pre, mask, valid_count))))
    first = low_back(jnp.einsum('ihwc,co->ihwo', shared, low(first_w), precision=highest))
    hidden = low(mask * jax.nn.silu(batch_norm(first, mask, valid_count)))
    second = low_back(jnp.einsum('ihwc,co->ihwo', hidden, low(second_w), precision=highest))
    gating = jax.nn.sigmoid(batch_norm(second, mask, valid_count))
    merged = low(gating * shared)
    conved = low_back(conv_three(merged, low(conv_w)))
    activ = mask * jax.nn.silu(batch_norm(conved, mask, valid_count))
    images, height, across, channels = activ.shape
    return activ.reshape(images, height // 2, 2, across // 2, 2, channels).mean(axis=(2, 4))

def pcgrad_weights(task_gram, flags):
    count_tasks = task_gram.shape[0]
    identity_rows = jnp.eye(count_tasks, dtype=jnp.float32)
    combined = jnp.zeros((count_tasks,), jnp.float32)
    for target in range(count_tasks):
        coeffs = identity_rows[target]
        for source in range(count_tasks):
            if source != target:
                inner_prod = jnp.sum(coeffs * task_gram[:, source])
                coeffs = coeffs - flags[target, source].astype(jnp.float32) * inner_prod / task_gram[source, source] * identity_rows[source]
        combined = combined + coeffs
    return combined

def orthogonalize(matrix):
    ortho = matrix / (jnp.sqrt(jnp.sum(matrix * matrix)) + 1e-07)
    for sweep in range(NS_STEPS):
        gram = jnp.einsum('kio,kip->op', ortho, ortho, precision=highest)
        combo = coeff_b * gram + coeff_c * jnp.dot(gram, gram, precision=highest)
        ortho = coeff_a * ortho + jnp.einsum('kip,po->kio', ortho, combo, precision=highest)
    return ortho

def reference(inputs, extents, conflicts, trunk_weight, attn_first, attn_second, branch_conv, trunk_momentum, first_momentum, second_momentum, conv_momentum, cotangent):
    images, height, across = (inputs.shape[0], inputs.shape[1], inputs.shape[2])
    rows_h = jnp.arange(height, dtype=jnp.int32)[None, :, None]
    cols_w = jnp.arange(across, dtype=jnp.int32)[None, None, :]
    mask = ((rows_h < extents[:, 0][:, None, None]) & (cols_w < extents[:, 1][:, None, None])).astype(jnp.float32)[..., None]
    valid_count = jnp.sum(mask)
    raw = inputs.astype(jnp.float32)
    forward = functools.partial(branch_forward, mask=mask, valid_count=valid_count)
    outputs = []
    input_grad = jnp.zeros(raw.shape, jnp.float32)
    trunk_grads, first_grads, second_grads, conv_grads = ([], [], [], [])
    for branch in range(TASKS):
        pooled, pull = jax.vjp(forward, raw, trunk_weight, attn_first[branch], attn_second[branch], branch_conv[branch])
        grads = pull(cotangent[branch].astype(jnp.float32))
        outputs.append(pooled.astype(jnp.bfloat16))
        input_grad = input_grad + grads[0]
        trunk_grads.append(grads[1])
        first_grads.append(grads[2])
        second_grads.append(grads[3])
        conv_grads.append(grads[4])
    trunk_stack = jnp.stack(trunk_grads)
    gram_raw = jnp.einsum('tkio,skio->ts', trunk_stack, trunk_stack, precision=highest)
    task_gram = gram_raw / jnp.float32(KK * C * C * IMAGES * H * W)
    combined = pcgrad_weights(gram_raw, conflicts)
    trunk_moment = moment_decay * trunk_momentum + jnp.einsum('t,tkio->kio', combined, trunk_stack, precision=highest)
    first_moment = moment_decay * first_momentum + jnp.stack(first_grads)
    second_moment = moment_decay * second_momentum + jnp.stack(second_grads)
    conv_moment = moment_decay * conv_momentum + jnp.stack(conv_grads)
    shrink = 1.0 - step_rate * weight_decay
    trunk_new = shrink * trunk_weight - step_rate * orthogonalize(trunk_moment)
    first_new = jnp.stack([shrink * attn_first[b] - step_rate * orthogonalize(first_moment[b][None])[0] for b in range(TASKS)])
    second_new = jnp.stack([shrink * attn_second[b] - step_rate * orthogonalize(second_moment[b][None])[0] for b in range(TASKS)])
    conv_new = jnp.stack([shrink * branch_conv[b] - step_rate * orthogonalize(conv_moment[b]) for b in range(TASKS)])
    return (jnp.stack(outputs), input_grad, trunk_new, first_new, second_new, conv_new, trunk_moment, first_moment, second_moment, conv_moment, task_gram)
```

```python
import functools

import jax
import jax.numpy as jnp
from jax import lax
from jax.experimental import pallas as pl
from jax.experimental.pallas import tpu as pltpu
from jax.sharding import PartitionSpec as P

NS_STEPS = 3

epsilon = 1e-05
moment_decay = 0.95
step_rate = 1.0
weight_decay = 0.01
shrink = 1.0 - step_rate * weight_decay
coeff_a = 3.4445
coeff_b = -4.775
coeff_c = 2.0315
bf16 = jnp.bfloat16
f32 = jnp.float32
i32 = jnp.int32

LANES = 128
TAPS = 9
STEPS = 4


ABS, REL, RING_ABS, RING_REL, ME = 0, 8, 16, 24, 32

RING = (0, 2, 4, 6, 7, 5, 3, 1)
OFFSETS = (0, -1, -2, -3, -4, 1, 2, 3)


def by_chip():
    return lax.axis_size("dp") == 8 and lax.axis_size("task") == 4


def make_table():
    if not by_chip():
        return jnp.zeros((64,), i32)
    me = lax.axis_index("task")
    index = lax.axis_index("dp")
    pos = (jnp.where(index % 2 == 0, index // 2, 7 - index // 2) + jnp.array(OFFSETS, i32) + 8) % 8
    places = jnp.stack([index ^ jnp.arange(8, dtype=i32), jnp.where(pos < 4, 2 * pos, 15 - 2 * pos)])
    mixed = ((places // 2) ^ me) * 2 + places % 2
    return jnp.concatenate([places[0], mixed[0], places[1], mixed[1], jnp.full((32,), me, i32)])


def ring_gather(shard):
    if not by_chip():
        return [lax.all_gather(shard, "dp", axis=shard.ndim - 2, tiled=True)]
    ahead, behind = [shard], [shard]
    for step in range(4):
        ahead.append(lax.ppermute(ahead[-1], "dp", [(RING[p], RING[(p + 1) % 8]) for p in range(8)]))
        if step < 3:
            behind.append(lax.ppermute(behind[-1], "dp", [(RING[p], RING[p - 1]) for p in range(8)]))
    return ahead + behind[1:]


def flip_dp(value, mask):
    return lax.ppermute(value, "dp", [(i, i ^ mask) for i in range(8)])


def gather_dp(shard):
    if not by_chip():
        return [lax.all_gather(shard, "dp", axis=shard.ndim - 2, tiled=True)]
    far = flip_dp(shard, 4)
    near = [flip_dp(shard, k) for k in (1, 2, 3)]
    return [shard] + near + [far] + [flip_dp(far, k) for k in (1, 2, 3)]


def scatter_dp(terms, deps=()):
    if not by_chip():
        (whole,) = terms
        copies = lax.axis_size("dp")
        whole = whole.reshape((copies, whole.shape[0] // copies) + whole.shape[1:]).astype(f32)
        return [lax.psum_scatter(whole, "dp", scatter_dimension=0, tiled=False)]
    got = [flip_dp(terms[4 + k], k) for k in (1, 2, 3)]
    near = terms[1:4]
    if deps:
        shape, dtype = terms[4].shape, terms[4].dtype
        beyond, *near = call(
            beyond_kernel,
            "beyond",
            [(v, WHOLE) for v in [terms[4]] + got] + [(v, REMAIN) for v in near],
            [(shape, dtype, WHOLE)] + [(shape, dtype, REMAIN)] * 3,
            us=1,
            deps=deps,
            aliases={4: 1, 5: 2, 6: 3},
        )
    else:
        beyond = (terms[4].astype(f32) + got[0].astype(f32)) + (got[1].astype(f32) + got[2].astype(f32))
    far = flip_dp(beyond.astype(terms[4].dtype), 4)
    return [terms[0]] + [flip_dp(v, k + 1) for k, v in enumerate(near)] + [far]


def beyond_kernel(term, g1, g2, g3, n1, n2, n3, out, o1, o2, o3):
    value = (term[...].astype(f32) + g1[...].astype(f32)) + (g2[...].astype(f32) + g3[...].astype(f32))
    out[...] = value.astype(out.dtype)


def wide_scatter(whole):
    copies = lax.axis_size("dp")
    whole = whole.reshape((copies, whole.shape[0] // copies) + whole.shape[1:])
    if not by_chip():
        whole = whole.astype(f32)
    return [lax.psum_scatter(whole, "dp", scatter_dimension=0, tiled=False)]


def exchange(values):
    if not by_chip():
        return lax.psum(values, "dp")
    near = [flip_dp(values, k) for k in (1, 2, 3)]
    half = (values + near[0]) + (near[1] + near[2])
    return half + flip_dp(half, 4)


def flip_task(value, mask):
    return lax.ppermute(value, "task", [(i, i ^ mask) for i in range(4)])


def gather_task(block):
    if not by_chip():
        whole = lax.all_gather(block, "task", axis=0, tiled=False)
        return [whole[t] for t in range(4)]
    core = flip_task(block, 1)
    chip = flip_task(block, 2)
    return [block, core, chip, flip_task(chip, 1)]


def route_task(blocks):
    if not by_chip():
        got = lax.all_to_all(jnp.stack(blocks), "task", 0, 0)
        return [got[t] for t in range(4)]
    return [blocks[0], flip_task(blocks[1], 1), flip_task(blocks[2], 2), flip_task(blocks[3], 3)]


def add_task(blocks):
    if not by_chip():
        return lax.psum_scatter(jnp.stack(blocks).astype(f32), "task", scatter_dimension=0, tiled=False)
    beyond = blocks[2].astype(f32) + flip_task(blocks[3], 1).astype(f32)
    near = blocks[0].astype(f32) + flip_task(blocks[1], 1).astype(f32)
    return near + flip_task(beyond.astype(bf16), 2).astype(f32)


WHOLE = pl.BlockSpec(memory_space=pltpu.VMEM)
SCALARS = pl.BlockSpec(memory_space=pltpu.SMEM)
REMAIN = pl.BlockSpec(memory_space=pl.ANY)


def room(shape, dtype, spec):
    if spec is SCALARS or spec is REMAIN:
        return 0
    dims = shape if spec is WHOLE else spec.block_shape
    size = jnp.dtype(dtype).itemsize
    dims = (1,) * (2 - len(dims)) + tuple(dims)
    lead = 1
    for d in dims[:-2]:
        lead *= d
    bytes_ = lead * -(-dims[-2] // 16) * 16 * -(-dims[-1] // LANES) * LANES * size
    return bytes_ if spec is WHOLE or spec.pipeline_mode is not None else 2 * bytes_


def call(kernel, name, ins, outs, scratch=(), grid=(), us=4.0, deps=(), aliases=None, spare=5):
    moved = sum(a.size * a.dtype.itemsize for a, _ in ins)
    shapes = [jax.ShapeDtypeStruct(s, d) for s, d, _ in outs]
    moved += sum(s.size * s.dtype.itemsize for s in shapes)
    need = spare * 1024 * 1024
    need += sum(room(a.shape, a.dtype, spec) for a, spec in ins) + sum(room(*out) for out in outs)
    need += sum(room(v.shape, v.dtype, WHOLE) for v in scratch if getattr(v, "memory_space", None) == pltpu.VMEM)
    skip = len(deps)
    return pl.pallas_call(
        lambda *refs: kernel(*refs[skip:]),
        name=name,
        grid=grid,
        in_specs=[REMAIN] * skip + [s for _, s in ins],
        out_specs=[s for _, _, s in outs],
        out_shape=shapes,
        scratch_shapes=list(scratch),
        input_output_aliases={skip + k: v for k, v in (aliases or {}).items()},
        compiler_params=pltpu.CompilerParams(vmem_limit_bytes=min(need, 58 * 1024 * 1024)),
        cost_estimate=pl.CostEstimate(flops=int(us * 0.3e9), bytes_accessed=int(moved), transcendentals=0),
    )(*deps, *[a for a, _ in ins])


def fixed(array):
    rank = array.ndim
    return (array, pl.BlockSpec(array.shape, lambda i: (0,) * rank, pipeline_mode=pl.Buffered(1)))


def now(array, rows):
    return (array, pl.BlockSpec((rows, array.shape[1]), lambda i: (jnp.minimum(i, STEPS - 1), 0)))


def before(array, rows):
    return (array, pl.BlockSpec((rows, array.shape[1]), lambda i: (jnp.maximum(i - 1, 0), 0)))


def out_now(rows, cols, count, dtype):
    return ((rows * count, cols), dtype, pl.BlockSpec((rows, cols), lambda i: (jnp.minimum(i, count - 1), 0)))


def out_before(rows, cols, count, dtype):
    return ((rows * count, cols), dtype, pl.BlockSpec((rows, cols), lambda i: (jnp.maximum(i - 1, 0), 0)))


def out_fixed(shape, dtype):
    return (shape, dtype, pl.BlockSpec(shape, lambda i: (0,) * len(shape)))


def wide(value, columns):
    return jnp.concatenate([value] * (columns // LANES), axis=1)


def fold(value):
    rows, columns = value.shape
    return jnp.sum(value.reshape(rows // 8, 8, columns), axis=0)


def edges(rows, across, columns):
    place = lax.broadcasted_iota(i32, (across, LANES), 0)
    first = jnp.where(place == 0, 0.0, 1.0)
    last = jnp.where(place == across - 1, 0.0, 1.0)
    return tuple(wide(jnp.concatenate([e] * (rows // across), axis=0), columns) for e in (first, last))


def step_back(value, first):
    return pltpu.roll(value, 1, axis=0) * first


def step_on(value, last):
    return pltpu.roll(value, value.shape[0] - 1, axis=0) * last


def sigmoid(value):
    return 0.5 * jnp.tanh(0.5 * value) + 0.5


def slope(value):
    sigma = sigmoid(value)
    return sigma * (1.0 + value * (1.0 - sigma))


def dot(a, b):
    return jnp.dot(a, b, preferred_element_type=f32)


def dot_last(a, b):
    return lax.dot_general(a, b, (((1,), (1,)), ((), ())), preferred_element_type=f32)


def dot_first(a, b):
    return lax.dot_general(a, b, (((0,), (0,)), ((), ())), preferred_element_type=f32)


def norm_terms(stats, trunk):
    total = jnp.sum(stats[...], axis=0)
    valid = wide(trunk[2:3, :], total.shape[1])
    mean = total[0:1] / valid
    return mean, lax.rsqrt(total[1:2] / valid - mean * mean + epsilon)


def back_terms(stats, trunk):
    total = jnp.sum(stats[...], axis=0)
    valid = wide(trunk[2:3, :], total.shape[1])
    return total[0:1] / valid, total[1:2] / valid


def put_rows(ref, acc):
    for k in range(ref.shape[1]):
        row = jnp.sum(acc[8 * k : 8 * k + 8, :], axis=0, keepdims=True)
        for j in range(ref.shape[0]):
            ref[j, k : k + 1, :] = row


def put_chunks(outs, table, first, whole):
    for k, out in enumerate(outs):
        size = out.shape[0]
        out[...] = whole[pl.ds(pl.multiple_of(table[first + k] * size, size), size), :].astype(out.dtype)


def place_chunks(chunks, table, first, dest, sems):
    copies = []
    for k, chunk in enumerate(chunks):
        rows = chunk.shape[-2]
        at = pl.ds(pl.multiple_of(table[first + k] * rows, rows), rows)
        slot = dest.at[at, :] if len(chunk.shape) == 2 else dest.at[:, at, :]
        copies.append(pltpu.make_async_copy(chunk, slot, sems.at[k]))
    return copies


def mask_kernel(rows, across, extents, mask):
    i = pl.program_id(0)
    place = lax.broadcasted_iota(i32, (across, LANES), 0)
    for line in range(rows // across):
        reach = jnp.where(i * (rows // across) + line < extents[0, 0], extents[0, 1], 0)
        mask[pl.ds(line * across, across), :] = jnp.where(place < reach, 1.0, 0.0)


def low_kernel(values, out):
    out[...] = values[...].astype(bf16)


def pair_low_kernel(first, second, out):
    columns = first.shape[1]
    out[:, 0:columns] = first[...].astype(bf16)
    out[:, columns:] = second[...].astype(bf16)


def turn_kernel(count, *rest):
    blocks, out = rest[:count], rest[-1]
    values = [b[...] for b in blocks]
    if len(rest) > count + 1:
        keep = rest[count][...].astype(bf16)
        values = [v * keep for v in values]
    out[...] = jnp.concatenate(values, axis=1).T


def trunk_kernel(rows, across, count, table, x0, x1, x2, x3, hide, mask, *rest):
    chunks = rest[:count]
    out, stats, weights, terms, acc, sems = rest[count:]
    i = pl.program_id(0)
    depth = terms.shape[1] // TAPS

    @pl.when(i == 0)
    def _():
        copies = place_chunks(chunks, table, RING_REL, weights, sems)
        for c in copies:
            c.start()
        terms[0:across, :] = jnp.zeros((across, terms.shape[1]), f32)
        terms[pl.ds(terms.shape[0] - across, across), :] = jnp.zeros((across, terms.shape[1]), f32)
        acc[...] = jnp.zeros_like(acc)
        for c in copies:
            c.wait()

    @pl.when(i < STEPS)
    def _():
        keep = hide[...].astype(bf16)
        values = jnp.concatenate([x[...] * keep for x in (x0, x1, x2, x3)], axis=1)
        terms[pl.ds(pl.multiple_of(across + i * rows, across), rows), :] = dot(values, weights[...])

    @pl.when(i > 0)
    def _():
        base = (i - 1) * rows
        first, last = edges(rows, across, depth)
        sides = []
        for b in range(3):
            side = None
            for a in range(3):
                at = pl.ds(pl.multiple_of(base + a * across, across), rows)
                term = terms[at, (3 * a + b) * depth : (3 * a + b + 1) * depth]
                side = term if side is None else side + term
            sides.append(side)
        value = sides[1] + step_back(sides[0], first) + step_on(sides[2], last)
        out[...] = value
        keep = mask[...]
        kept = value * keep
        acc[0:8, :] += fold(kept)
        acc[8:16, :] += fold(kept * value)
        acc[16:24, :] += fold(keep)

    @pl.when(i == STEPS)
    def _():
        put_rows(stats, acc)


def shared_kernel(pre, stats, mask, part, trunk):
    total = jnp.sum(stats[...], axis=0)
    valid = total[2:3]
    mean = total[0:1] / valid
    inverse = lax.rsqrt(total[1:2] / valid - mean * mean + epsilon)
    trunk[0:1, :] = mean
    trunk[1:2, :] = inverse
    trunk[2:3, :] = valid
    trunk[3:8, :] = jnp.zeros((5, LANES), f32)
    normed = (pre[...] - mean) * inverse
    part[...] = (mask[...] * normed * sigmoid(normed)).astype(bf16)


def first_kernel(count, table, x0, x1, x2, x3, mask, *rest):
    chunks = rest[:count]
    pre, shared, stats, kept_weights, weights, acc, sems = rest[count:]
    i = pl.program_id(0)

    @pl.when(i == 0)
    def _():
        copies = place_chunks(chunks, table, RING_ABS, kept_weights, sems)
        for c in copies:
            c.start()
        acc[...] = jnp.zeros_like(acc)
        for c in copies:
            c.wait()
        for r in range(4):
            at = pl.ds(pl.multiple_of((table[ME] ^ r) * LANES, LANES), LANES)
            weights[r * LANES : (r + 1) * LANES, :] = kept_weights[at, 0 : pre.shape[1]]

    blocks = [x0[...], x1[...], x2[...], x3[...]]
    me = table[ME]
    for r, block in enumerate(blocks):
        shared[:, pl.ds(pl.multiple_of((me ^ r) * LANES, LANES), LANES)] = block
    value = dot(jnp.concatenate(blocks, axis=1), weights[...])
    pre[...] = value
    kept = value * wide(mask[...], value.shape[1])
    acc[0:8, :] += fold(kept)
    acc[8:16, :] += fold(kept * value)

    @pl.when(i == STEPS - 1)
    def _():
        put_rows(stats, acc)


def second_kernel(pre, mask, stats1, trunk, weights, out, hidden, stats, acc):
    i = pl.program_id(0)

    @pl.when(i == 0)
    def _():
        acc[...] = jnp.zeros_like(acc)

    mean, inverse = norm_terms(stats1, trunk)
    keep = wide(mask[...], pre.shape[1])
    normed = (pre[...] - mean) * inverse
    low = (keep * normed * sigmoid(normed)).astype(bf16)
    hidden[...] = low
    value = dot(low, weights[:, out.shape[1] :])
    out[...] = value
    kept = value * keep
    acc[0:8, :] += fold(kept)
    acc[8:16, :] += fold(kept * value)

    @pl.when(i == STEPS - 1)
    def _():
        put_rows(stats, acc)


def clear_ends(padded, across):
    zero = jnp.zeros((across, padded.shape[1]), padded.dtype)
    padded[0:across, :] = zero
    padded[pl.ds(padded.shape[0] - across, across), :] = zero


def branch_kernel(rows, across, count, table, pre, shared, stats2, trunk, mask, *rest):
    chunks = rest[:count]
    out, merged, stats, weights, sides, acc, sems = rest[count:]
    i = pl.program_id(0)
    depth = pre.shape[1]
    copies = place_chunks(chunks, table, ABS, weights, sems)

    @pl.when(i == 0)
    def _():
        for c in copies:
            c.start()
        clear_ends(sides, across)
        acc[...] = jnp.zeros_like(acc)

    @pl.when(i < STEPS)
    def _():
        mean, inverse = norm_terms(stats2, trunk)
        gate = sigmoid((pre[...] - mean) * inverse)
        low = (gate * shared[...].astype(f32)).astype(bf16)
        merged[...] = low
        first, last = edges(rows, across, depth)
        value = low.astype(f32)
        at = pl.ds(pl.multiple_of(across + i * rows, across), rows)
        sides[at, 0:depth] = step_back(value, first).astype(bf16)
        sides[at, depth : 2 * depth] = low
        sides[at, 2 * depth : 3 * depth] = step_on(value, last).astype(bf16)

    @pl.when(i == 1)
    def _():
        for c in copies:
            c.wait()

    @pl.when(i > 0)
    def _():
        base = (i - 1) * rows
        value = None
        for a in range(3):
            at = pl.ds(pl.multiple_of(base + a * across, across), rows)
            term = dot(sides[at, :], weights[3 * a : 3 * a + 3].reshape(3 * depth, depth))
            value = term if value is None else value + term
        out[...] = value
        kept = value * wide(mask[...], depth)
        acc[0:8, :] += fold(kept)
        acc[8:16, :] += fold(kept * value)

    @pl.when(i == STEPS)
    def _():
        put_rows(stats, acc)


def pool_kernel(pre, cot, spread, mask, stats4, trunk, features, grad, stats, acc):
    i = pl.program_id(0)

    @pl.when(i == 0)
    def _():
        acc[...] = jnp.zeros_like(acc)

    mean, inverse = norm_terms(stats4, trunk)
    keep = wide(mask[...], pre.shape[1])
    normed = (pre[...] - mean) * inverse
    sigma = sigmoid(normed)
    active = keep * normed * sigma
    high = active.astype(bf16)
    low = (active - high.astype(f32)).astype(bf16)
    ups = spread[...]
    pooled = dot_first(ups, high) + dot_first(ups, low)
    features[...] = (0.25 * pooled).astype(bf16)
    value = dot(ups, cot[...]) * 0.25 * keep * (sigma * (1.0 + normed * (1.0 - sigma)))
    grad[...] = value
    acc[0:8, :] += fold(value)
    acc[8:16, :] += fold(value * normed)

    @pl.when(i == STEPS - 1)
    def _():
        put_rows(stats, acc)


def branch_back_kernel(
    rows, across, count, table, pre, grad, mask, stats4, back4, trunk, pre2, shared, stats2, *rest
):
    chunks = rest[:count]
    delta, gate_grad, shared_grad, stats, weights, sides, acc, sems = rest[count:]
    i = pl.program_id(0)
    depth = pre.shape[1]
    copies = place_chunks(chunks, table, ABS, weights, sems)

    @pl.when(i == 0)
    def _():
        for c in copies:
            c.start()
        clear_ends(sides, across)
        acc[...] = jnp.zeros_like(acc)

    @pl.when(i < STEPS)
    def _():
        mean, inverse = norm_terms(stats4, trunk)
        one, two = back_terms(back4, trunk)
        keep = wide(mask[...], depth)
        normed = (pre[...] - mean) * inverse
        low = (inverse * (grad[...] - keep * (one + normed * two))).astype(bf16)
        delta[...] = low
        first, last = edges(rows, across, depth)
        value = low.astype(f32)
        at = pl.ds(pl.multiple_of(across + i * rows, across), rows)
        sides[at, 0:depth] = step_on(value, last).astype(bf16)
        sides[at, depth : 2 * depth] = low
        sides[at, 2 * depth : 3 * depth] = step_back(value, first).astype(bf16)

    @pl.when(i == 1)
    def _():
        for c in copies:
            c.wait()

    @pl.when(i > 0)
    def _():
        base = (i - 1) * rows
        value = None
        for a in range(3):
            at = pl.ds(pl.multiple_of(base + (2 - a) * across, across), rows)
            for b in range(3):
                term = dot_last(sides[at, b * depth : (b + 1) * depth], weights[3 * a + b])
                value = term if value is None else value + term
        mean, inverse = norm_terms(stats2, trunk)
        normed = (pre2[...] - mean) * inverse
        gate = sigmoid(normed)
        shared_grad[...] = value * gate
        inner = value * shared[...].astype(f32) * (gate * (1.0 - gate))
        gate_grad[...] = inner
        acc[0:8, :] += fold(inner)
        acc[8:16, :] += fold(inner * normed)

    @pl.when(i == STEPS)
    def _():
        put_rows(stats, acc)


def branch_weight_kernel(rows, across, count, table, delta, turned, *rest):
    outs = rest[:count]
    sides, whole = rest[count:]
    i = pl.program_id(0)
    depth = delta.shape[1]
    pixels = turned.shape[1]

    @pl.when(i == 0)
    def _():
        clear_ends(sides, across)

    @pl.when(i < STEPS)
    def _():
        first, last = edges(rows, across, depth)
        low = delta[...]
        value = low.astype(f32)
        at = pl.ds(pl.multiple_of(across + i * rows, across), rows)
        sides[at, 0:depth] = step_on(value, last).astype(bf16)
        sides[at, depth : 2 * depth] = low
        sides[at, 2 * depth : 3 * depth] = step_back(value, first).astype(bf16)

    @pl.when(i >= STEPS)
    def _():
        at = pl.ds(pl.multiple_of((2 - (i - STEPS)) * across, across), pixels)
        whole[...] = dot(turned[...], sides[at, :])
        put_chunks(outs, table, ABS, whole)


def second_back_kernel(
    gate_grad, pre2, pre1, mask, back2, stats2, stats1, trunk, weights, delta, grad, stats, acc
):
    i = pl.program_id(0)
    depth = pre1.shape[1]

    @pl.when(i == 0)
    def _():
        acc[...] = jnp.zeros_like(acc)

    keep = wide(mask[...], depth)
    mean, inverse = norm_terms(stats2, trunk)
    one, two = back_terms(back2, trunk)
    normed = (pre2[...] - mean) * inverse
    low = (inverse * (gate_grad[...] - keep * (one + normed * two))).astype(bf16)
    delta[...] = low
    mean, inverse = norm_terms(stats1, trunk)
    normed = (pre1[...] - mean) * inverse
    value = dot_last(low, weights[:, depth:]) * keep * slope(normed)
    grad[...] = value
    acc[0:8, :] += fold(value)
    acc[8:16, :] += fold(value * normed)

    @pl.when(i == STEPS - 1)
    def _():
        put_rows(stats, acc)


def first_back_kernel(
    table, grad, pre1, mask, back1, stats1, trunk, shared_grad, weights, delta, b0, b1, b2, b3, whole
):
    depth = pre1.shape[1]

    keep = wide(mask[...], depth)
    mean, inverse = norm_terms(stats1, trunk)
    one, two = back_terms(back1, trunk)
    normed = (pre1[...] - mean) * inverse
    low = (inverse * (grad[...] - keep * (one + normed * two))).astype(bf16)
    delta[...] = low
    whole[...] = (shared_grad[...] + dot_last(low, weights[:, 0:depth])).astype(bf16)
    me = table[ME]
    for r, block in enumerate((b0, b1, b2, b3)):
        block[...] = whole[:, pl.ds(pl.multiple_of((me ^ r) * LANES, LANES), LANES)]


def pair_weight_kernel(count, table, shared, delta1, hidden, delta2, *rest):
    outs = rest[:count]
    (whole,) = rest[count:]
    depth = shared.shape[1]
    whole[:, 0:depth] = dot_first(shared[...], delta1[...])
    whole[:, depth:] = dot_first(hidden[...], delta2[...])
    put_chunks(outs, table, ABS, whole)


def trunk_sums_kernel(g0, g1, g2, g3, pre, mask, trunk, stats, acc):
    i = pl.program_id(0)

    @pl.when(i == 0)
    def _():
        acc[...] = jnp.zeros_like(acc)

    normed = (pre[...] - trunk[0:1, :]) * trunk[1:2, :]
    scale = mask[...] * slope(normed)
    for r, g in enumerate((g0, g1, g2, g3)):
        value = g[...].astype(f32) * scale
        acc[16 * r : 16 * r + 8, :] += fold(value)
        acc[16 * r + 8 : 16 * r + 16, :] += fold(value * normed)

    @pl.when(i == STEPS - 1)
    def _():
        put_rows(stats, acc)


def trunk_weight_kernel(
    rows, across, count, table, g0, g1, g2, g3, pre, mask, trunk, back, turned, *rest
):
    outs = rest[:count]
    delta, sides, whole = rest[count:]
    i = pl.program_id(0)
    depth = 4 * LANES
    pixels = turned.shape[1]

    @pl.when(i == 0)
    def _():
        clear_ends(sides, across)

    @pl.when(i < STEPS)
    def _():
        mean, inverse, valid = trunk[0:1, :], trunk[1:2, :], trunk[2:3, :]
        normed = (pre[...] - mean) * inverse
        keep = mask[...]
        scale = keep * slope(normed)
        total = jnp.sum(back[...], axis=0) / valid
        lows = []
        for r, g in enumerate((g0, g1, g2, g3)):
            value = g[...].astype(f32) * scale
            value = inverse * (value - keep * (total[2 * r : 2 * r + 1] + normed * total[2 * r + 1 : 2 * r + 2]))
            lows.append(value.astype(bf16))
        delta[...] = sum(low.astype(f32) for low in lows).astype(bf16)
        low = jnp.concatenate(lows, axis=1)
        first, last = edges(rows, across, depth)
        value = low.astype(f32)
        at = pl.ds(pl.multiple_of(across + i * rows, across), rows)
        sides[at, 0:depth] = step_on(value, last).astype(bf16)
        sides[at, depth : 2 * depth] = low
        sides[at, 2 * depth : 3 * depth] = step_back(value, first).astype(bf16)

    @pl.when(i >= STEPS)
    def _():
        at = pl.ds(pl.multiple_of((2 - (i - STEPS)) * across, across), pixels)
        whole[...] = dot(turned[...], sides[at, :])
        put_chunks(outs, table, REL, whole)


def input_kernel(rows, across, delta, weights, b0, b1, b2, b3, sides):
    i = pl.program_id(0)
    depth = delta.shape[1]

    @pl.when(i == 0)
    def _():
        clear_ends(sides, across)

    @pl.when(i < STEPS)
    def _():
        first, last = edges(rows, across, depth)
        low = delta[...]
        value = low.astype(f32)
        at = pl.ds(pl.multiple_of(across + i * rows, across), rows)
        sides[at, 0:depth] = step_on(value, last).astype(bf16)
        sides[at, depth : 2 * depth] = low
        sides[at, 2 * depth : 3 * depth] = step_back(value, first).astype(bf16)

    @pl.when(i > 0)
    def _():
        base = (i - 1) * rows
        value = None
        for a in range(3):
            at = pl.ds(pl.multiple_of(base + (2 - a) * across, across), rows)
            term = dot_last(sides[at, :], weights[:, 3 * a * depth : 3 * (a + 1) * depth])
            value = term if value is None else value + term
        for r, block in enumerate((b0, b1, b2, b3)):
            block[...] = value[:, r * LANES : (r + 1) * LANES].astype(bf16)


def trunk_total_kernel(count, copies, table, *rest):
    terms = rest[:count]
    total, grams = rest[count:]
    value = sum(t[...].astype(f32) for t in terms)
    total[...] = value
    me = table[ME]
    for r in range(4):
        for s in range(r, 4):
            part = None
            for tap in range(TAPS):
                left = value[:, (4 * tap + r) * LANES : (4 * tap + r + 1) * LANES]
                right = value[:, (4 * tap + s) * LANES : (4 * tap + s + 1) * LANES]
                part = left * right if part is None else part + left * right
            entry = jnp.sum(fold(part), axis=0, keepdims=True)
            entry = jnp.broadcast_to(jnp.sum(entry, axis=1, keepdims=True), (1, LANES))
            for j in range(copies):
                grams[j, pl.ds((me ^ r) * 4 + (me ^ s), 1), :] = entry
                if r != s:
                    grams[j, pl.ds((me ^ s) * 4 + (me ^ r), 1), :] = entry


def trunk_moment_kernel(table, flags, gram, total, momentum, moment, low, rest):
    entry = [[gram[4 * t + s : 4 * t + s + 1, :] for s in range(4)] for t in range(4)]
    combined = [jnp.zeros((1, LANES), f32) for _ in range(4)]
    for target in range(4):
        coeffs = [jnp.full((1, LANES), 1.0 if t == target else 0.0, f32) for t in range(4)]
        for source in range(4):
            if source != target:
                inner = sum(coeffs[t] * entry[t][source] for t in range(4))
                flag = flags[target, source].astype(f32)
                coeffs[source] = coeffs[source] - flag * inner / entry[source][source]
        combined = [combined[t] + coeffs[t] for t in range(4)]
    me = table[ME]
    mixed = []
    for r in range(4):
        mixed.append(sum(jnp.where((me ^ r) == t, combined[t], 0.0) for t in range(4)))
    values = []
    for tap in range(TAPS):
        value = moment_decay * momentum[tap]
        for r in range(4):
            value = value + mixed[r] * total[:, (4 * tap + r) * LANES : (4 * tap + r + 1) * LANES]
        moment[tap] = value
        values.append(value)
    low[...], rest[...] = split(jnp.concatenate(values, axis=0))


def trunk_gram_kernel(table, m0, m1, m2, m3, whole, parts):
    me = table[ME]
    for r, m in enumerate((m0, m1, m2, m3)):
        whole[:, pl.ds(pl.multiple_of((me ^ r) * LANES, LANES), LANES)] = m[...]
    value = dot_first(m0[...], whole[...])
    size = parts.shape[1]
    for d in range(parts.shape[0]):
        parts[d] = value[d * size : (d + 1) * size]


def spread_kernel(parts, out):
    value = jnp.sum(parts[...], axis=0)
    for d in range(out.shape[0]):
        out[d] = value


def split(value):
    high = value.astype(bf16)
    return high, (value - high.astype(f32)).astype(bf16)


def dot_split(a, b):
    return dot(a[0], b[0]) + (dot(a[0], b[1]) + dot(a[1], b[0]))


def dot_even(a, b):
    left = jnp.concatenate([a[0], a[0], a[1]], axis=1)
    right = jnp.concatenate([b[0], b[1], b[0]], axis=0)
    half = left.shape[0] // 2
    top = dot(left[:half], right)
    corner = dot(left[half:], right[:, half:])
    return jnp.concatenate([top, jnp.concatenate([top[:, half:].T, corner], axis=1)], axis=0)


def newton_schulz(gram, place=None):
    size = gram.shape[0]
    same = lax.broadcasted_iota(i32, (size, size), 0) == lax.broadcasted_iota(i32, (size, size), 1)
    diagonal = jnp.sum(fold(jnp.where(same, gram, 0.0)), axis=0, keepdims=True)
    norm = jnp.sqrt(jnp.sum(diagonal, axis=1, keepdims=True)) + 1e-07
    scale = 1.0 / norm
    value = gram * (scale * scale)
    product = None
    for sweep in range(NS_STEPS):
        parts = split(value)
        step = coeff_b * value + coeff_c * dot_even(parts, parts) + jnp.where(same, coeff_a, 0.0)
        if sweep < NS_STEPS - 1:
            pair = split(step)
            value = dot_even(split(dot_even(pair, parts)), pair)
            product = pair if sweep == 0 else split(dot_even(product, pair))
    if place is not None:
        return dot_split(product, split(place(step))) * scale
    return dot_even(product, split(step)) * scale


def trunk_new_kernel(table, g0, g1, g2, g3, r0, r1, r2, r3, whole, weight, out, gram, last, rest):
    me = table[ME]
    for r, g in enumerate((g0, g1, g2, g3)):
        gram[pl.ds(pl.multiple_of((me ^ r) * LANES, LANES), LANES), :] = g[...]
    for r, m in enumerate((r0, r1, r2, r3)):
        rest[:, pl.ds(pl.multiple_of((me ^ r) * LANES, LANES), LANES)] = m[...]
    own = pl.ds(pl.multiple_of(table[ME + 1] * LANES, LANES), LANES)

    def place(step):
        last[...] = step
        return last[:, own]

    turn = newton_schulz(gram[...], place)
    value = dot_split((whole[...], rest[...]), split(turn))
    depth = weight.shape[1]
    for tap in range(TAPS):
        out[tap] = shrink * weight[tap] - step_rate * value[tap * depth : (tap + 1) * depth]


def conv_moment_kernel(count, table, *rest):
    terms = rest[:count]
    momentum, moment, *parts, gram = rest[count:]
    columns = momentum.shape[2]
    lows = []
    for tap in range(TAPS):
        at = slice(tap * columns, (tap + 1) * columns)
        value = moment_decay * momentum[tap] + sum(t[:, at].astype(f32) for t in terms)
        moment[tap] = value
        lows.append(value)
    low = jnp.concatenate(lows, axis=0).astype(bf16)
    gram[...] = dot_first(low, low)
    put_chunks(parts, table, ABS, gram)


def conv_new_kernel(count, table, *rest):
    chunks = rest[:count]
    moment, weight, out, gram, sems = rest[count:]
    copies = place_chunks(chunks, table, ABS, gram, sems)
    for c in copies:
        c.start()
    for c in copies:
        c.wait()
    turn = newton_schulz(gram[...])
    value = dot_split(split(moment[...]), split(turn))
    depth = weight.shape[1]
    for tap in range(TAPS):
        out[tap] = shrink * weight[tap] - step_rate * value[tap * depth : (tap + 1) * depth]


def pair_moment_kernel(count, *rest):
    terms = rest[:count]
    momentum1, momentum2, moment1, moment2, low = rest[count:]
    columns = momentum1.shape[1]
    value = sum(t[...].astype(f32) for t in terms)
    one = moment_decay * momentum1[...] + value[:, 0:columns]
    two = moment_decay * momentum2[...] + value[:, columns:]
    moment1[...] = one
    moment2[...] = two
    low[:, 0:columns] = one.astype(bf16)
    low[:, columns:] = two.astype(bf16)


def pair_new_kernel(*refs):
    chunks, (moment1, moment2, weight1, weight2, out1, out2) = refs[:-6], refs[-6:]
    columns = weight1.shape[1]
    every = jnp.concatenate([c[...] for c in chunks], axis=0)
    for k, (moment, weight, out) in enumerate(((moment1, weight1, out1), (moment2, weight2, out2))):
        half = every[:, k * columns : (k + 1) * columns]
        turn = newton_schulz(dot_first(half, half))
        out[...] = shrink * weight[...] - step_rate * dot_split(split(moment[...]), split(turn))


def body(
    inputs,
    extents,
    conflicts,
    trunk_weight,
    attn_first,
    attn_second,
    branch_conv,
    trunk_momentum,
    first_momentum,
    second_momentum,
    conv_momentum,
    cotangent,
):
    height, across = (inputs.shape[1], inputs.shape[2])
    pixels = height * across
    rows = pixels // STEPS
    depth, width = trunk_weight.shape[1], trunk_weight.shape[2]
    channels = attn_first.shape[2]
    devices = lax.axis_size("dp")
    n = 1
    table = make_table()
    scal = (table, SCALARS)
    slots = 8 if by_chip() else 1

    def dma(count):
        return pltpu.SemaphoreType.DMA((count,))

    def remain(chunks):
        return [(c, REMAIN) for c in chunks]

    def vmem(*shape, dtype=f32):
        return pltpu.VMEM(shape, dtype)

    full_in = gather_task(inputs.reshape(pixels, width))
    trunk_chunks = ring_gather(jnp.swapaxes(trunk_weight.astype(bf16), 0, 1).reshape(depth, TAPS * width))
    (pair_low,) = call(
        pair_low_kernel,
        "pair_low",
        [(attn_first[0], WHOLE), (attn_second[0], WHOLE)],
        [((depth, 2 * channels), bf16, WHOLE)],
        us=1,
    )
    pair_chunks = ring_gather(pair_low)
    (conv_low,) = call(
        low_kernel,
        "low",
        [(branch_conv[0], WHOLE)],
        [((TAPS, depth, channels), bf16, WHOLE)],
        us=1.5,
    )
    conv_chunks = [lax.all_gather(conv_low, "dp", axis=1, tiled=True)]
    whole_table = (jnp.zeros((8,), i32), SCALARS)
    count = len(trunk_chunks)
    (mask,) = call(
        functools.partial(mask_kernel, rows, across),
        "mask",
        [(extents, SCALARS)],
        [out_now(rows, width, STEPS, f32)],
        grid=(STEPS,),
        us=2,
    )
    trunk_pre, sums, trunk_weights = call(
        functools.partial(trunk_kernel, rows, across, count),
        "trunk",
        [scal] + [now(x, rows) for x in full_in] + [now(mask, rows), before(mask, rows)] + remain(trunk_chunks),
        [
            out_before(rows, width, STEPS, f32),
            out_fixed((n, 3, width), f32),
            out_fixed((channels, TAPS * width), bf16),
        ],
        [
            vmem(pixels + 2 * across, TAPS * width),
            vmem(24, width),
            dma(count),
        ],
        (STEPS + 1,),
        us=7,
        deps=[pair_chunks[2], pair_chunks[6]] if by_chip() else [],
    )
    sums = exchange(sums)
    shared_part, trunk = call(
        shared_kernel,
        "shared",
        [now(trunk_pre, rows), fixed(sums), now(mask, rows)],
        [out_now(rows, width, STEPS, bf16), out_fixed((8, width), f32)],
        grid=(STEPS,),
        us=3,
        deps=[pair_chunks[3], pair_chunks[7]] if by_chip() else [],
    )
    shared_blocks = gather_task(shared_part)

    first_pre, shared, sums, weights = call(
        functools.partial(first_kernel, count),
        "first",
        [scal] + [now(x, rows) for x in shared_blocks] + [now(mask, rows)] + remain(pair_chunks),
        [
            out_now(rows, channels, STEPS, f32),
            out_now(rows, channels, STEPS, bf16),
            out_fixed((n, 2, channels), f32),
            out_fixed((channels, 2 * channels), bf16),
        ],
        [vmem(channels, channels, dtype=bf16), vmem(16, channels), dma(count)],
        (STEPS,),
        us=6,
    )
    stats1 = exchange(sums)
    second_pre, hidden, sums = call(
        second_kernel,
        "second",
        [now(first_pre, rows), now(mask, rows), fixed(stats1), fixed(trunk), fixed(weights)],
        [
            out_now(rows, channels, STEPS, f32),
            out_now(rows, channels, STEPS, bf16),
            out_fixed((n, 2, channels), f32),
        ],
        [vmem(16, channels)],
        (STEPS,),
        us=6,
        spare=36,
    )
    stats2 = exchange(sums)
    sides = vmem(pixels + 2 * across, 3 * channels, dtype=bf16)
    conv_pre, merged, sums = call(
        functools.partial(branch_kernel, rows, across, 1),
        "branch",
        [
            whole_table,
            now(second_pre, rows),
            now(shared, rows),
            fixed(stats2),
            fixed(trunk),
            before(mask, rows),
        ]
        + remain(conv_chunks),
        [
            out_before(rows, channels, STEPS, f32),
            out_now(rows, channels, STEPS, bf16),
            out_fixed((n, 2, channels), f32),
        ],
        [vmem(TAPS, channels, channels, dtype=bf16), sides, vmem(16, channels), dma(1)],
        (STEPS + 1,),
        us=13,
        spare=30,
    )
    stats4 = exchange(sums)

    def turn(blocks, hide, name):
        return call(
            functools.partial(turn_kernel, len(blocks)),
            name,
            [now(v, rows) for v in blocks] + [now(v, rows) for v in hide],
            [((channels, pixels), bf16, pl.BlockSpec((channels, rows), lambda i: (0, i)))],
            grid=(STEPS,),
            us=3,
        )[0]

    pool_rows = rows // 4
    line = jnp.arange(rows) // across
    spot = (line // 2) * (across // 2) + (jnp.arange(rows) % across) // 2
    spread = (spot[:, None] == jnp.arange(pool_rows)[None, :]).astype(bf16)
    features, grad, sums = call(
        pool_kernel,
        "pool",
        [
            now(conv_pre, rows),
            now(cotangent.reshape(pixels // 4, channels), pool_rows),
            fixed(spread),
            now(mask, rows),
            fixed(stats4),
            fixed(trunk),
        ],
        [
            out_now(pool_rows, channels, STEPS, bf16),
            out_now(rows, channels, STEPS, f32),
            out_fixed((n, 2, channels), f32),
        ],
        [vmem(16, channels)],
        (STEPS,),
        us=6,
    )
    back4 = exchange(sums)
    conv_delta, gate_grad, shared_grad, sums = call(
        functools.partial(branch_back_kernel, rows, across, 1),
        "branch_back",
        [
            whole_table,
            now(conv_pre, rows),
            now(grad, rows),
            now(mask, rows),
            fixed(stats4),
            fixed(back4),
            fixed(trunk),
            before(second_pre, rows),
            before(shared, rows),
            fixed(stats2),
        ]
        + remain(conv_chunks),
        [
            out_now(rows, channels, STEPS, bf16),
            out_before(rows, channels, STEPS, f32),
            out_before(rows, channels, STEPS, f32),
            out_fixed((n, 2, channels), f32),
        ],
        [vmem(TAPS, channels, channels, dtype=bf16), sides, vmem(16, channels), dma(1)],
        (STEPS + 1,),
        us=15,
    )
    back2 = exchange(sums)
    merged_turned = turn([merged], [], "merged_turn")
    (conv_term,) = call(
        functools.partial(branch_weight_kernel, rows, across, 1),
        "branch_weight",
        [whole_table, now(conv_delta, rows), fixed(merged_turned)],
        [
            (
                (channels, TAPS * channels),
                bf16,
                pl.BlockSpec((channels, 3 * channels), lambda i: (0, jnp.maximum(i - STEPS, 0))),
            )
        ],
        [sides, vmem(channels, 3 * channels)],
        (STEPS + 3,),
        us=10,
    )
    conv_parts = wide_scatter(conv_term)
    second_delta, first_grad, sums = call(
        second_back_kernel,
        "second_back",
        [
            now(gate_grad, rows),
            now(second_pre, rows),
            now(first_pre, rows),
            now(mask, rows),
            fixed(back2),
            fixed(stats2),
            fixed(stats1),
            fixed(trunk),
            fixed(weights),
        ],
        [
            out_now(rows, channels, STEPS, bf16),
            out_now(rows, channels, STEPS, f32),
            out_fixed((n, 2, channels), f32),
        ],
        [vmem(16, channels)],
        (STEPS,),
        us=5,
        spare=36,
        deps=[conv_term],
    )
    back1 = exchange(sums)
    first_delta, *blocks = call(
        first_back_kernel,
        "first_back",
        [
            scal,
            now(first_grad, rows),
            now(first_pre, rows),
            now(mask, rows),
            fixed(back1),
            fixed(stats1),
            fixed(trunk),
            now(shared_grad, rows),
            fixed(weights),
        ],
        [out_now(rows, channels, STEPS, bf16)] + [out_now(rows, width, STEPS, bf16)] * 4,
        [vmem(rows, channels, dtype=bf16)],
        (STEPS,),
        us=4,
    )
    routed = route_task(blocks)
    pair_terms = call(
        functools.partial(pair_weight_kernel, slots),
        "pair_weight",
        [scal] + [(v, WHOLE) for v in (shared, first_delta, hidden, second_delta)],
        [((channels // slots, 2 * channels), bf16, WHOLE)] * slots,
        [vmem(channels, 2 * channels)],
        us=3,
        deps=routed[1:2],
    )

    pair_parts = scatter_dp(pair_terms)
    first_moment, second_moment, pair_low = call(
        functools.partial(pair_moment_kernel, len(pair_parts)),
        "pair_moment",
        [(v, WHOLE) for v in pair_parts] + [(first_momentum[0], WHOLE), (second_momentum[0], WHOLE)],
        [
            ((depth, channels), f32, WHOLE),
            ((depth, channels), f32, WHOLE),
            ((depth, 2 * channels), bf16, WHOLE),
        ],
        us=2,
    )
    pair_moments = gather_dp(pair_low)

    (sums,) = call(
        trunk_sums_kernel,
        "trunk_sums",
        [now(g, rows) for g in routed] + [now(trunk_pre, rows), now(mask, rows), fixed(trunk)],
        [out_fixed((n, 8, width), f32)],
        [vmem(64, width)],
        (STEPS,),
        us=2,
    )
    back0 = exchange(sums)
    input_turned = turn(full_in, [mask], "input_turn")
    chunk = channels // slots
    *trunk_terms, delta_total = call(
        functools.partial(trunk_weight_kernel, rows, across, slots),
        "trunk_weight",
        [scal]
        + [now(g, rows) for g in routed]
        + [now(trunk_pre, rows), now(mask, rows), fixed(trunk), fixed(back0), fixed(input_turned)],
        [
            (
                (chunk, TAPS * 4 * width),
                bf16,
                pl.BlockSpec((chunk, 12 * width), lambda i: (0, jnp.maximum(i - STEPS, 0))),
            )
        ]
        * slots
        + [out_now(rows, width, STEPS, bf16)],
        [vmem(pixels + 2 * across, 12 * width, dtype=bf16), vmem(channels, 12 * width)],
        (STEPS + 3,),
        us=6,
        deps=pair_moments[1:],
    )
    input_blocks = call(
        functools.partial(input_kernel, rows, across),
        "input",
        [now(delta_total, rows), fixed(trunk_weights)],
        [out_before(rows, width, STEPS, bf16)] * 4,
        [vmem(pixels + 2 * across, 3 * width, dtype=bf16)],
        (STEPS + 1,),
        us=6,
    )
    conv_moment, *conv_grams = call(
        functools.partial(conv_moment_kernel, len(conv_parts)),
        "conv_moment",
        [scal] + [(v.reshape(depth, -1), WHOLE) for v in conv_parts] + [(conv_momentum[0], WHOLE)],
        [((TAPS, depth, channels), f32, WHOLE)] + [((channels // slots, channels), f32, WHOLE)] * slots,
        [vmem(channels, channels)],
        us=3,
        deps=trunk_terms[:1],
    )
    trunk_parts = scatter_dp(trunk_terms, deps=[input_blocks[0]])
    input_grad = (add_task(input_blocks) * mask).reshape(inputs.shape)

    if by_chip():
        conv_grams = scatter_dp(conv_grams)
        conv_gram = (conv_grams[0] + conv_grams[1]) + (conv_grams[2] + conv_grams[3]) + conv_grams[4]
        conv_grams = gather_dp(conv_gram)
    else:
        conv_gram = lax.psum(conv_grams[0], "dp")
        conv_grams = [conv_gram]
    first_new, second_new = call(
        pair_new_kernel,
        "pair_new",
        [(v, WHOLE) for v in pair_moments]
        + [(v, WHOLE) for v in (first_moment, second_moment, attn_first[0], attn_second[0])],
        [((depth, channels), f32, WHOLE)] * 2,
        us=18,
    )
    (conv_new,) = call(
        functools.partial(conv_new_kernel, len(conv_grams)),
        "conv_new",
        [scal]
        + remain(conv_grams)
        + [(v, WHOLE) for v in (conv_moment.reshape(TAPS * depth, channels), branch_conv[0])],
        [((TAPS, depth, channels), f32, WHOLE)],
        [vmem(channels, channels), dma(len(conv_grams))],
        us=11,
        spare=44,
    )

    everyone = 4 * devices if by_chip() else 1
    trunk_total, grams = call(
        functools.partial(trunk_total_kernel, len(trunk_parts), everyone),
        "trunk_total",
        [scal] + [(v, WHOLE) for v in trunk_parts],
        [((depth, TAPS * 4 * width), f32, WHOLE), ((everyone, 16, width), f32, WHOLE)],
        us=3,
        deps=[first_new] if by_chip() else [],
    )
    if by_chip():
        grams = lax.all_to_all(grams, ("dp", "task"), 0, 0)
        gram_rows = jnp.sum(grams, axis=0)
    else:
        gram_rows = lax.psum(grams[0], ("dp", "task"))
    all_pixels = inputs.shape[0] * devices * pixels
    task_gram = gram_rows[:, 0].reshape(4, 4) / jnp.float32(TAPS * channels * channels * all_pixels)
    trunk_moment, trunk_low, trunk_rest = call(
        trunk_moment_kernel,
        "trunk_moment",
        [scal, (conflicts, SCALARS), (gram_rows, WHOLE), (trunk_total, WHOLE), (trunk_momentum, WHOLE)],
        [((TAPS, depth, width), f32, WHOLE)] + [((TAPS * depth, width), bf16, WHOLE)] * 2,
        us=2.5,
        deps=[conv_gram] if by_chip() else [],
    )
    lows = gather_task(trunk_low)
    rests = gather_task(trunk_rest)
    if by_chip():
        trunk_whole, trunk_part = call(
            trunk_gram_kernel,
            "trunk_gram",
            [scal] + [(v, WHOLE) for v in lows],
            [
                ((TAPS * depth, channels), bf16, WHOLE),
                ((devices, width // devices, channels), f32, WHOLE),
            ],
            us=2,
        )
        trunk_part = lax.all_to_all(trunk_part, "dp", 0, 0)
        (gram_own,) = call(
            spread_kernel,
            "trunk_gram_own",
            [(trunk_part, WHOLE)],
            [((devices, width // devices, channels), f32, WHOLE)],
            us=1,
            deps=conv_grams[1:5] + rests[1:],
        )
        gram_blocks = gather_task(lax.all_to_all(gram_own, "dp", 0, 0).reshape(width, channels))
    else:
        trunk_whole = jnp.concatenate(lows, axis=1)
        trunk_part = jnp.einsum("ro,rp->op", trunk_low, trunk_whole, preferred_element_type=f32)
        gram_blocks = gather_task(lax.psum(trunk_part, "dp"))
    (trunk_new,) = call(
        trunk_new_kernel,
        "trunk_new",
        [(table.at[ME + 1].set(lax.axis_index("task")), SCALARS)]
        + [(v, WHOLE) for v in gram_blocks + rests + [trunk_whole, trunk_weight]],
        [((TAPS, depth, width), f32, WHOLE)],
        [vmem(channels, channels), vmem(channels, channels), vmem(TAPS * depth, channels, dtype=bf16)],
        us=11,
        deps=[conv_new] if by_chip() else [],
    )
    return (
        features.reshape(cotangent.shape),
        input_grad,
        trunk_new,
        first_new[None],
        second_new[None],
        conv_new[None],
        trunk_moment,
        first_moment[None],
        second_moment[None],
        conv_moment[None],
        task_gram,
    )


def solution(mesh):
    placed = (
        P("dp", None, None, "task"),
        P("dp", None),
        P(),
        P(None, "dp", "task"),
        P("task", "dp", None),
        P("task", "dp", None),
        P("task", None, "dp", None),
        P(None, "dp", "task"),
        P("task", "dp", None),
        P("task", "dp", None),
        P("task", None, "dp", None),
        P("task", "dp", None, None, None),
    )
    return jax.shard_map(
        body,
        mesh=mesh,
        in_specs=placed,
        out_specs=(
            P("task", "dp", None, None, None),
            P("dp", None, None, "task"),
            P(None, "dp", "task"),
            P("task", "dp", None),
            P("task", "dp", None),
            P("task", None, "dp", None),
            P(None, "dp", "task"),
            P("task", "dp", None),
            P("task", "dp", None),
            P("task", None, "dp", None),
            P(),
        ),
        check_vma=False,
    )
```
